32 devices in a mesh: wide: 8 (over z, y), sub: 4 (over x, core).
Axes of the slice: x: 2, y: 2, z: 4, core: 2. Of those that a mesh axis runs over, the one named last changes fastest.
Arguments:
- lengths: int32 [4, 1024], P('sub', 'wide'), may hold values from 0 to 2048, as said below
- postings: bfloat16 [4, 16384, 128], P('sub', 'wide'), may hold values from -6 to 6
- codes: int32 [4, 8, 16384], P('sub', None, 'wide'), may hold values from 0 to 255
- rotation: bfloat16 [128, 128], replicated, may hold values from -0.5 to 0.5
Outputs:
- rotated_slices: bfloat16 [4, 128, 8192], P(None, 'sub', 'wide')
- codebook: float32 [8, 16, 256], P('sub')
The draws below stay inside these ranges and needn't reach their ends.
Inputs may be any that keep to these rules, and one draw needn't show every extreme that they name: Each slab's lengths add up to 8192; no device holds more than 2048 rows in all; in each slab some device holds exactly 2048 rows, all in one list; lengths and whole devices may be empty.
All inputs are finite; a program needn't handle non-finite values.
Results may differ from the reference program's by a relative error of at most 0.0029.
Values may be sent and summed in bfloat16 or wider, within the bound.
A program may use at most 128 MiB of HBM per device.

```python
import jax
import jax.numpy as jnp

D = 128
M = 8
KCODES = 256
ROWS_DEV = 1024
LISTS_DEV = 128
CAP = 2048
SUBDIM = 16
SLAB = 8192
N_WIDE = 8
N_SUB = 4


def one_slab(key):
    key_far, key_short, key_full, key_flip, key_cut = jax.random.split(key, 5)
    half_count = N_WIDE // 2
    far_rows = jax.random.randint(key_far, (), 1, ROWS_DEV + 1).astype(jnp.int32)
    spare = (ROWS_DEV - far_rows).astype(jnp.int32)
    inner = jax.random.randint(key_short, (half_count - 2,), 0, spare + 1).astype(jnp.int32)
    inner = jnp.sort(inner)
    edges = jnp.concatenate([jnp.zeros((1,), jnp.int32), inner, jnp.reshape(spare, (1,))])
    parts = (edges[1:] - edges[:-1]).astype(jnp.int32)
    chosen = jax.random.randint(key_full, (), 0, half_count).astype(jnp.int32)
    slots = jnp.arange(half_count, dtype=jnp.int32)
    source = jnp.clip(slots - (slots > chosen).astype(jnp.int32), 0, half_count - 2)
    deficits = jnp.where(slots == chosen, 0, parts[source]).astype(jnp.int32)
    upper = (2 * ROWS_DEV - deficits).astype(jnp.int32)
    lower = jnp.concatenate([jnp.reshape(spare, (1,)), jnp.zeros((half_count - 1,), jnp.int32)])
    totals = jnp.concatenate([lower, upper]).astype(jnp.int32)
    flip = jax.random.randint(key_flip, (), 0, 2).astype(jnp.int32)
    totals = jnp.where(flip == 1, totals[::-1], totals).astype(jnp.int32)
    cuts = jax.random.randint(key_cut, (N_WIDE, LISTS_DEV - 1), 0, totals[:, None] + 1).astype(jnp.int32)
    cuts = jnp.sort(cuts, axis=1)
    full_device = totals == 2 * ROWS_DEV
    cuts = jnp.where(full_device[:, None], 0, cuts).astype(jnp.int32)
    bounds = jnp.concatenate([jnp.zeros((N_WIDE, 1), jnp.int32), cuts, totals[:, None]], axis=1)
    return (bounds[:, 1:] - bounds[:, :-1]).reshape(-1)


def draw_lengths(key, part):
    keys = jax.random.split(key, N_SUB)
    return jax.vmap(one_slab)(keys).astype(jnp.int32)


def set_ends(entries, key, low, top_value):
    index_at = [jax.random.randint(jax.random.fold_in(key, axis), (), 0, length) for axis, length in enumerate(entries.shape)]
    main_axis = entries.shape.index(max(entries.shape))
    next_to = index_at[:main_axis] + [(index_at[main_axis] + 1) % entries.shape[main_axis]] + index_at[main_axis + 1:]
    return entries.at[tuple(index_at)].set(low).at[tuple(next_to)].set(top_value)


def block_scale(own_key, extent, cuts, least, high):
    gain = 1.0
    for axis_at, shards_of in cuts:
        draws = jax.random.uniform(jax.random.fold_in(jax.random.fold_in(own_key, 6), axis_at), (shards_of,), jnp.float32, least / len(cuts), high / len(cuts))
        gain = gain * jnp.repeat(jnp.exp(draws), extent[axis_at] // shards_of).reshape((-1,) + (1,) * (len(extent) - 1 - axis_at))
    return gain


def noise(own_key, extent, width, bound, cuts=(), kind=jnp.bfloat16):
    entries = width * jax.random.normal(own_key, extent, jnp.float32)
    if cuts:
        entries = entries * block_scale(own_key, extent, cuts, -0.22, 0.18)
    return jnp.clip(entries, -bound, bound).astype(kind)


def setup_inputs(seed: int = 0) -> dict:
    splits = jax.random.split(jax.random.key(seed), 5)
    lengths = draw_lengths(jax.random.fold_in(splits[4], 71), 0)
    postings = noise(splits[1], (N_SUB, N_WIDE * CAP, D), 1.0, 6.0, ((0, 4), (1, 8)))
    codes = set_ends(jax.random.randint(splits[2], (N_SUB, M, N_WIDE * CAP), 0, KCODES), jax.random.fold_in(splits[2], 1), 0, KCODES - 1).astype(jnp.int32)
    rotation = noise(splits[3], (D, D), D ** -0.5, 0.5)
    return {"lengths": lengths, "postings": postings, "codes": codes, "rotation": rotation}


def reference(lengths, postings, codes, rotation):
    totals = jnp.sum(lengths.reshape(N_SUB, N_WIDE, LISTS_DEV), axis=2).astype(jnp.int32)
    ends = jnp.cumsum(totals, axis=1).astype(jnp.int32)
    starts = (ends - totals).astype(jnp.int32)
    position = jnp.arange(SLAB, dtype=jnp.int32)
    rotated_all = []
    codes_all = []
    for group in range(N_SUB):
        owner = jnp.sum((ends[group][:, None] <= position[None, :]).astype(jnp.int32), axis=0).astype(jnp.int32)
        owner = jnp.minimum(owner, N_WIDE - 1)
        index = (owner * CAP + position - starts[group][owner]).astype(jnp.int32)
        rows = postings[group][index]
        rotated = jnp.dot(rows, rotation, preferred_element_type=jnp.float32).astype(jnp.bfloat16)
        rotated_all.append(rotated)
        codes_all.append(codes[group][:, index])
    rotated_all = jnp.stack(rotated_all)
    codes_all = jnp.stack(codes_all)
    rotated_slices = jnp.transpose(rotated_all, (0, 2, 1))
    books = []
    for sub_index in range(M):
        values = rotated_all[:, :, sub_index * SUBDIM:(sub_index + 1) * SUBDIM].astype(jnp.float32).reshape(-1, SUBDIM)
        labels = codes_all[:, sub_index, :].reshape(-1)
        sums = jax.ops.segment_sum(values, labels, KCODES)
        counts = jax.ops.segment_sum(jnp.ones(labels.shape, jnp.float32), labels, KCODES)
        books.append((sums / (counts[:, None] + 1.0)).T)
    return rotated_slices, jnp.stack(books)
```

```python
import functools

import jax
import jax.numpy as jnp
from jax import lax
from jax.experimental import pallas as pl
from jax.experimental.pallas import tpu as pltpu
from jax.sharding import PartitionSpec as P

KCODES = 256
SUBDIM = 16
LANES = 128
CODE_ROWS = 16
MESH = pl.DeviceIdType.MESH
NT = (((1,), (1,)), ((), ()))


def when(condition):
    if condition is True:
        return lambda body: body()
    return pl.when(condition)


def kernel(
    n_wide,
    n_sub,
    len_ref,
    post_ref,
    code_ref,
    rot_ref,
    out_ref,
    book_ref,
    lens,
    local,
    halves,
    arrived,
    final,
    slices,
    acc,
    parts,
    parts_in,
    tile,
    tiles_in,
    len_send,
    len_recv,
    wide_send,
    wide_recv,
    sub_send,
    sub_recv,
    part_send,
    part_recv,
    tile_send,
    tile_recv,
):
    me = lax.axis_index("wide")
    sub = lax.axis_index("sub")
    stages = n_wide.bit_length() - 1
    capacity, dims = post_ref.shape[1], post_ref.shape[2]
    spaces = code_ref.shape[1]
    shard = capacity // 2
    chunks, height, width = halves.shape[2:]
    own_dims = dims // n_sub
    own_spaces = spaces // n_sub
    n_tiles = parts.shape[0]
    columns = KCODES // LANES

    def wide_peer(distance):
        return lax.rem(me + distance, n_wide)

    def sub_peer(distance):
        return lax.rem(sub + distance, n_sub)

    barrier = pltpu.get_barrier_semaphore()
    for d in range(1, n_wide):
        pl.semaphore_signal(barrier, inc=1, device_id=(wide_peer(d), sub), device_id_type=MESH)
    for d in range(1, n_sub):
        pl.semaphore_signal(barrier, inc=1, device_id=(me, sub_peer(d)), device_id_type=MESH)
    pl.semaphore_wait(barrier, n_wide + n_sub - 2)

    len_copies = []
    for d in range(1, n_wide):
        copy = pltpu.make_async_remote_copy(
            src_ref=len_ref,
            dst_ref=lens.at[me],
            send_sem=len_send.at[d],
            recv_sem=len_recv.at[d],
            device_id=(wide_peer(d), sub),
            device_id_type=MESH,
        )
        copy.start()
        len_copies.append(copy)
    lens[me] = len_ref[...]

    turned = rot_ref[...].astype(jnp.float32).T.astype(jnp.bfloat16)
    blocks = capacity // LANES
    step = capacity // 4
    for i in range(4):
        span = slice(i * step, (i + 1) * step)
        block = lax.dot_general(turned, post_ref[0, span, :], NT, preferred_element_type=jnp.float32)
        block = block.astype(jnp.bfloat16)
        for k in range(step // LANES):
            local[i * (step // LANES) + k, :dims] = block[:, k * LANES : (k + 1) * LANES]
    spare = jnp.zeros((height - dims - spaces, LANES), jnp.float32)
    for k in range(blocks):
        labels = code_ref[0, :, k * LANES : (k + 1) * LANES].astype(jnp.float32)
        local[k, dims:] = jnp.concatenate([labels, spare], axis=0).astype(jnp.bfloat16)

    for copy in len_copies:
        copy.wait_recv()
    all_lens = lens[...].reshape(n_wide, lens.shape[2])
    device = lax.broadcasted_iota(jnp.int32, all_lens.shape, 0)

    def start_of(index):
        return jnp.sum(jnp.where(device < index, all_lens, 0))

    mine = start_of(me)
    rest = lax.rem(n_wide * capacity - mine, LANES)
    across = lax.broadcasted_iota(jnp.int32, (2 * LANES, LANES), 0) - lax.broadcasted_iota(
        jnp.int32, (2 * LANES, LANES), 1
    )
    shift = jnp.where(across == rest, 1.0, 0.0).astype(jnp.bfloat16)

    def placed(half):
        first = lax.rem(half * shard - mine + n_wide * capacity, capacity) // LANES
        loaded = [local[lax.rem(first + k, blocks)] for k in range(shard // LANES + 1)]
        pairs = [jnp.concatenate(loaded[k : k + 2], axis=1) for k in range(shard // LANES)]
        moved = jnp.dot(
            jnp.concatenate(pairs, axis=0), shift, preferred_element_type=jnp.float32
        ).astype(jnp.bfloat16)
        moved = [moved[k * height : (k + 1) * height] for k in range(shard // LANES)]
        each = width // LANES
        return [jnp.concatenate(moved[q * each : (q + 1) * each], axis=1) for q in range(chunks)]

    def bit(j):
        return lax.rem(me // (1 << j), 2)

    wide_copies = {}

    def send_wide(j, q):
        copy = pltpu.make_async_remote_copy(
            src_ref=halves.at[j, 0, q],
            dst_ref=arrived.at[j, q],
            send_sem=wide_send.at[j, q],
            recv_sem=wide_recv.at[j, q],
            device_id=(me + (1 << j) - (2 << j) * bit(j), sub),
            device_id_type=MESH,
        )
        copy.start()
        wide_copies[j, q] = copy

    for q, piece in enumerate(placed(1 - bit(0))):
        halves[0, 0, q] = piece
        send_wide(0, q)
    for q, piece in enumerate(placed(bit(0))):
        halves[0, 1, q] = piece

    edges = []
    for j in range(stages):
        group = me - lax.rem(me, 2 << j)
        edges.append((start_of(group), start_of(group + (1 << j))))

    lane = lax.broadcasted_iota(jnp.int32, (height, width), 1)

    def pick(j, q, position):
        below = jnp.where(position < edges[j][1], 1, 0) + bit(j)
        return jnp.where(below == 1, halves[j, 1, q], arrived[j, q])

    sub_copies = {}

    def advance(j, q):
        wide_copies[j, q].wait_recv()
        if j < stages - 1:
            low = lax.rem(me, 2 << j) * shard + q * width
            first = edges[j][0]

            def position(half):
                offset = half * ((2 << j) * shard) + low - first
                return first + jnp.bitwise_and(offset + lane, (4 << j) * shard - 1)

            halves[j + 1, 0, q] = pick(j, q, position(1 - bit(j + 1)))
            send_wide(j + 1, q)
            halves[j + 1, 1, q] = pick(j, q, position(bit(j + 1)))
            return
        rows = pick(j, q, me * shard + q * width + lane)
        for s in range(n_sub):
            final[q, s, :own_dims] = rows[s * own_dims : (s + 1) * own_dims]
            final[q, s, own_dims:] = rows[dims:]
        for d in range(1, n_sub):
            copy = pltpu.make_async_remote_copy(
                src_ref=final.at[q, sub_peer(d)],
                dst_ref=slices.at[q, sub],
                send_sem=sub_send.at[q, d],
                recv_sem=sub_recv.at[q, d],
                device_id=(me, sub_peer(d)),
                device_id_type=MESH,
            )
            copy.start()
            sub_copies[q, d] = copy

    centroid = lax.broadcasted_iota(jnp.int32, (KCODES, n_sub * width), 0).astype(jnp.float32)
    code_row = lax.broadcasted_iota(jnp.int32, (CODE_ROWS, n_sub * width), 0)

    def refit(q):
        span = slice(q * width, (q + 1) * width)
        pieces = []
        for d in range(n_sub):
            slab = sub_peer(n_sub - d)
            if d:
                sub_copies[q, d].wait_recv()
                piece = slices[q, slab]
            else:
                piece = final[q, slab]
            out_ref[slab, :, span] = piece[:own_dims]
            pieces.append(piece)
        values = jnp.concatenate([piece[:own_dims] for piece in pieces], axis=1)
        labels = jnp.concatenate([piece[own_dims:] for piece in pieces], axis=1).astype(jnp.float32)
        ones = jnp.ones((SUBDIM, n_sub * width), jnp.bfloat16)
        for space in range(own_spaces):
            label = jnp.sum(
                jnp.where(code_row == sub * own_spaces + space, labels, 0.0), axis=0, keepdims=True
            )
            onehot = jnp.where(centroid == label, 1.0, 0.0).astype(jnp.bfloat16)
            left = jnp.concatenate([values[space * SUBDIM : (space + 1) * SUBDIM], ones], axis=0)
            part = lax.dot_general(left, onehot, NT, preferred_element_type=jnp.float32)
            acc[space] = part if q == 0 else acc[space] + part

    for turn in range(chunks + stages):
        for j in reversed(range(stages + 1)):
            q = turn - j
            if 0 <= q < chunks:
                if j < stages:
                    advance(j, q)
                else:
                    refit(q)

    def where_is(t):
        space, rest = divmod(t, 2 * columns)
        row, column = divmod(rest, columns)
        return space, row * 8, slice(column * LANES, (column + 1) * LANES)

    for t in range(n_tiles):
        space, row, span = where_is(t)
        parts[t, :8] = acc[space, row : row + 8, span]
        parts[t, 8:] = acc[space, SUBDIM : SUBDIM + 8, span]

    every = n_tiles == n_wide

    def owner(index):
        return True if every else index < n_tiles

    part_copies = []
    for d in range(1, n_wide):
        peer = wide_peer(d)
        copy = pltpu.make_async_remote_copy(
            src_ref=parts.at[peer if every else lax.rem(peer, n_tiles)],
            dst_ref=parts_in.at[me],
            send_sem=part_send.at[d],
            recv_sem=part_recv.at[d],
            device_id=(peer, sub),
            device_id_type=MESH,
        )
        when(owner(peer))(copy.start)
        part_copies.append((peer, copy))

    tile_copies = []
    for d in range(1, n_wide):
        slot = me if every else lax.rem(me, n_tiles)
        copy = pltpu.make_async_remote_copy(
            src_ref=tile,
            dst_ref=tiles_in.at[slot],
            send_sem=tile_send.at[d],
            recv_sem=tile_recv.at[d],
            device_id=(wide_peer(d), sub),
            device_id_type=MESH,
        )
        tile_copies.append((wide_peer(n_wide - d), copy))

    def add_up():
        slot = me if every else lax.rem(me, n_tiles)
        total = parts[slot]
        for d, (peer, copy) in enumerate(part_copies, 1):
            copy.wait_recv()
            total = total + parts_in[wide_peer(n_wide - d)]
        value = total[:8] / (total[8:] + 1.0)
        tile[...] = value
        for source, copy in tile_copies:
            copy.start()
        tiles_in[slot] = value

    when(owner(me))(add_up)
    for source, copy in tile_copies:
        when(owner(source))(copy.wait_recv)
    for t in range(n_tiles):
        space, row, span = where_is(t)
        book_ref[space, row : row + 8, span] = tiles_in[t]

    for copy in [*len_copies, *wide_copies.values(), *sub_copies.values()]:
        copy.wait_send()
    for peer, copy in part_copies:
        when(owner(peer))(copy.wait_send)

    def drain():
        for source, copy in tile_copies:
            copy.wait_send()

    when(owner(me))(drain)


def solution(mesh):
    n_wide, n_sub = mesh.shape["wide"], mesh.shape["sub"]
    stages = n_wide.bit_length() - 1

    def body(lengths, postings, codes, rotation):
        capacity, dims = postings.shape[1:]
        spaces = codes.shape[1]
        shard = capacity // 2
        width = 256
        chunks = shard // width
        height = dims + CODE_ROWS
        own_dims, own_spaces = dims // n_sub, spaces // n_sub
        n_tiles = own_spaces * (SUBDIM // 8) * (KCODES // LANES)
        bf16, f32 = jnp.bfloat16, jnp.float32
        vmem = pl.BlockSpec(memory_space=pltpu.VMEM)
        dma = pltpu.SemaphoreType.DMA
        return pl.pallas_call(
            functools.partial(kernel, n_wide, n_sub),
            out_shape=(
                jax.ShapeDtypeStruct((n_sub, own_dims, shard), bf16),
                jax.ShapeDtypeStruct((own_spaces, SUBDIM, KCODES), f32),
            ),
            in_specs=[vmem] * 4,
            out_specs=(vmem, vmem),
            scratch_shapes=[
                pltpu.VMEM((n_wide, *lengths.shape), jnp.int32),
                pltpu.VMEM((capacity // LANES, height, LANES), bf16),
                pltpu.VMEM((stages, 2, chunks, height, width), bf16),
                pltpu.VMEM((stages, chunks, height, width), bf16),
                pltpu.VMEM((chunks, n_sub, own_dims + CODE_ROWS, width), bf16),
                pltpu.VMEM((chunks, n_sub, own_dims + CODE_ROWS, width), bf16),
                pltpu.VMEM((own_spaces, 2 * SUBDIM, KCODES), f32),
                pltpu.VMEM((n_tiles, 16, LANES), f32),
                pltpu.VMEM((n_wide, 16, LANES), f32),
                pltpu.VMEM((8, LANES), f32),
                pltpu.VMEM((n_tiles, 8, LANES), f32),
                dma((n_wide,)),
                dma((n_wide,)),
                dma((stages, chunks)),
                dma((stages, chunks)),
                dma((chunks, n_sub)),
                dma((chunks, n_sub)),
                dma((n_wide,)),
                dma((n_wide,)),
                dma((n_wide,)),
                dma((n_wide,)),
            ],
            compiler_params=pltpu.CompilerParams(
                collective_id=0, has_side_effects=True, vmem_limit_bytes=32 * 1024 * 1024
            ),
        )(lengths, postings, codes, rotation)

    return jax.shard_map(
        body,
        mesh=mesh,
        in_specs=(P("sub", "wide"), P("sub", "wide", None), P("sub", None, "wide"), P()),
        out_specs=(P(None, "sub", "wide"), P("sub", None, None)),
        check_vma=False,
    )
```

```python
import functools

import jax
import jax.numpy as jnp
from jax import lax
from jax.experimental import pallas as pl
from jax.experimental.pallas import tpu as pltpu
from jax.sharding import PartitionSpec as P

KCODES = 256
SUBDIM = 16
LANES = 128
MESH = pl.DeviceIdType.MESH
NT = (((1,), (1,)), ((), ()))


def when(condition):
    if condition is True:
        return lambda body: body()
    return pl.when(condition)


def kernel(
    n_wide,
    n_sub,
    len_ref,
    post_hbm,
    code_hbm,
    rot_hbm,
    out_ref,
    book_ref,
    post_ref,
    code_ref,
    rot_ref,
    lens,
    local,
    halves,
    arrived,
    final,
    sums,
    sums_in,
    acc,
    parts,
    parts_in,
    tile,
    tiles_in,
    len_send,
    len_recv,
    wide_send,
    wide_recv,
    sub_send,
    sub_recv,
    sum_send,
    sum_recv,
    part_send,
    part_recv,
    tile_send,
    tile_recv,
    load,
):
    me = lax.axis_index("wide")
    sub = lax.axis_index("sub")
    stages = n_wide.bit_length() - 1
    capacity, dims = post_ref.shape[1], post_ref.shape[2]
    spaces = code_ref.shape[1]
    shard = capacity // 2
    chunks, height, width = halves.shape[2:]
    own_dims = dims // n_sub
    own_spaces = spaces // n_sub
    n_tiles = parts.shape[0]
    columns = KCODES // LANES

    def wide_peer(distance):
        return lax.rem(me + distance, n_wide)

    def sub_peer(distance):
        return lax.rem(sub + distance, n_sub)

    loads = [
        pltpu.make_async_copy(source, target, load.at[i])
        for i, (source, target) in enumerate(
            ((rot_hbm, rot_ref), (post_hbm, post_ref), (code_hbm, code_ref), (len_ref, lens.at[me]))
        )
    ]
    for copy in loads:
        copy.start()
    barrier = pltpu.get_barrier_semaphore()
    for d in range(1, n_wide):
        pl.semaphore_signal(barrier, inc=1, device_id=(wide_peer(d), sub), device_id_type=MESH)
    for d in range(1, n_sub):
        pl.semaphore_signal(barrier, inc=1, device_id=(me, sub_peer(d)), device_id_type=MESH)
    pl.semaphore_wait(barrier, n_wide + n_sub - 2)

    len_copies = []
    for d in range(1, n_wide):
        copy = pltpu.make_async_remote_copy(
            src_ref=len_ref,
            dst_ref=lens.at[me],
            send_sem=len_send.at[d],
            recv_sem=len_recv.at[d],
            device_id=(wide_peer(d), sub),
            device_id_type=MESH,
        )
        copy.start()
        len_copies.append(copy)

    loads[0].wait()
    turned = rot_ref[...].astype(jnp.float32).T.astype(jnp.bfloat16)
    blocks = capacity // LANES
    step = capacity // 4
    loads[1].wait()
    for i in range(4):
        span = slice(i * step, (i + 1) * step)
        block = lax.dot_general(turned, post_ref[0, span, :], NT, preferred_element_type=jnp.float32)
        block = block.astype(jnp.bfloat16)
        for k in range(step // LANES):
            local[i * (step // LANES) + k] = block[:, k * LANES : (k + 1) * LANES]
    loads[2].wait()
    loads[3].wait()
    for copy in len_copies:
        copy.wait_recv()
    all_lens = lens[...].reshape(n_wide, lens.shape[2])
    device = lax.broadcasted_iota(jnp.int32, all_lens.shape, 0)

    def start_of(index):
        return jnp.sum(jnp.where(device < index, all_lens, 0))

    mine = start_of(me)
    rest = lax.rem(n_wide * capacity - mine, LANES)
    across = lax.broadcasted_iota(jnp.int32, (2 * LANES, LANES), 0) - lax.broadcasted_iota(
        jnp.int32, (2 * LANES, LANES), 1
    )
    shift = jnp.where(across == rest, 1.0, 0.0).astype(jnp.bfloat16)

    def placed(half):
        first = lax.rem(half * shard - mine + n_wide * capacity, capacity) // LANES
        loaded = [local[lax.rem(first + k, blocks)] for k in range(shard // LANES + 1)]
        pairs = [jnp.concatenate(loaded[k : k + 2], axis=1) for k in range(shard // LANES)]
        moved = jnp.dot(
            jnp.concatenate(pairs, axis=0), shift, preferred_element_type=jnp.float32
        ).astype(jnp.bfloat16)
        moved = [moved[k * height : (k + 1) * height] for k in range(shard // LANES)]
        each = width // LANES
        return [jnp.concatenate(moved[q * each : (q + 1) * each], axis=1) for q in range(chunks)]

    def bit(j):
        return lax.rem(me // (1 << j), 2)

    wide_copies = {}

    def send_wide(j, q):
        copy = pltpu.make_async_remote_copy(
            src_ref=halves.at[j, 0, q],
            dst_ref=arrived.at[j, q],
            send_sem=wide_send.at[j, q],
            recv_sem=wide_recv.at[j, q],
            device_id=(me + (1 << j) - (2 << j) * bit(j), sub),
            device_id_type=MESH,
        )
        copy.start()
        wide_copies[j, q] = copy

    for q, piece in enumerate(placed(1 - bit(0))):
        halves[0, 0, q] = piece
        send_wide(0, q)
    for q, piece in enumerate(placed(bit(0))):
        halves[0, 1, q] = piece

    edges = []
    for j in range(stages):
        group = me - lax.rem(me, 2 << j)
        edges.append((start_of(group), start_of(group + (1 << j))))

    lane = lax.broadcasted_iota(jnp.int32, (height, width), 1)

    def pick(j, q, position):
        below = jnp.where(position < edges[j][1], 1, 0) + bit(j)
        return jnp.where(below == 1, halves[j, 1, q], arrived[j, q])

    sub_copies = {}

    def advance(j, q):
        wide_copies[j, q].wait_recv()
        if j < stages - 1:
            low = lax.rem(me, 2 << j) * shard + q * width
            first = edges[j][0]

            def position(half):
                offset = half * ((2 << j) * shard) + low - first
                return first + jnp.bitwise_and(offset + lane, (4 << j) * shard - 1)

            halves[j + 1, 0, q] = pick(j, q, position(1 - bit(j + 1)))
            send_wide(j + 1, q)
            halves[j + 1, 1, q] = pick(j, q, position(bit(j + 1)))
            return
        rows = pick(j, q, me * shard + q * width + lane)
        for s in range(n_sub):
            final[q, s] = rows[s * own_dims : (s + 1) * own_dims]
        span = pl.ds(q * width, width)
        for d in range(1, n_sub):
            copy = pltpu.make_async_remote_copy(
                src_ref=final.at[q, sub_peer(d)],
                dst_ref=out_ref.at[sub, :, span],
                send_sem=sub_send.at[q, d],
                recv_sem=sub_recv.at[q, d],
                device_id=(me, sub_peer(d)),
                device_id_type=MESH,
            )
            copy.start()
            sub_copies[q, d] = copy
        out_ref[sub, :, span] = final[q, sub]

    pieces = 4
    part_slots = capacity // pieces
    centroid = lax.broadcasted_iota(jnp.int32, (KCODES, part_slots), 0)
    slot = lax.broadcasted_iota(jnp.int32, (spaces, capacity), 1)
    ones = jnp.ones((SUBDIM, part_slots), jnp.bfloat16)
    code_ref[0] = jnp.where(slot < start_of(me + 1) - mine, code_ref[0], -1)

    def refit(space):
        total = None
        for i in range(pieces):
            span = slice(i * part_slots, (i + 1) * part_slots)
            labels = code_ref[0, space : space + 1, span]
            onehot = jnp.where(centroid == labels, 1.0, 0.0).astype(jnp.bfloat16)
            each = part_slots // LANES
            values = [
                local[i * each + k, space * SUBDIM : (space + 1) * SUBDIM] for k in range(each)
            ]
            left = jnp.concatenate([jnp.concatenate(values, axis=1), ones], axis=0)
            part = lax.dot_general(left, onehot, NT, preferred_element_type=jnp.float32)
            total = part if total is None else total + part
        sums[space // own_spaces, space % own_spaces] = total[: SUBDIM + 8]

    sum_copies = []

    def send_sums():
        for d in range(1, n_sub):
            copy = pltpu.make_async_remote_copy(
                src_ref=sums.at[sub_peer(d)],
                dst_ref=sums_in.at[sub],
                send_sem=sum_send.at[d],
                recv_sem=sum_recv.at[d],
                device_id=(me, sub_peer(d)),
                device_id_type=MESH,
            )
            copy.start()
            sum_copies.append(copy)

    def where_is(t):
        space, rest = divmod(t, 2 * columns)
        row, column = divmod(rest, columns)
        return space, row * 8, slice(column * LANES, (column + 1) * LANES)

    every = n_tiles == n_wide

    def owner(index):
        return True if every else index < n_tiles

    part_copies = []

    def send_parts():
        for d, copy in enumerate(sum_copies, 1):
            copy.wait_recv()
        total = sums[sub]
        for d in range(1, n_sub):
            total = total + sums_in[sub_peer(n_sub - d)]
        acc[...] = total
        for t in range(n_tiles):
            space, row, span = where_is(t)
            parts[t, :8] = acc[space, row : row + 8, span]
            parts[t, 8:] = acc[space, SUBDIM : SUBDIM + 8, span]
        for d in range(1, n_wide):
            peer = wide_peer(d)
            copy = pltpu.make_async_remote_copy(
                src_ref=parts.at[peer if every else lax.rem(peer, n_tiles)],
                dst_ref=parts_in.at[me],
                send_sem=part_send.at[d],
                recv_sem=part_recv.at[d],
                device_id=(peer, sub),
                device_id_type=MESH,
            )
            when(owner(peer))(copy.start)
            part_copies.append((peer, copy))

    tile_copies = []
    for d in range(1, n_wide):
        slot = me if every else lax.rem(me, n_tiles)
        copy = pltpu.make_async_remote_copy(
            src_ref=tile,
            dst_ref=tiles_in.at[slot],
            send_sem=tile_send.at[d],
            recv_sem=tile_recv.at[d],
            device_id=(wide_peer(d), sub),
            device_id_type=MESH,
        )
        tile_copies.append((wide_peer(n_wide - d), copy))

    def add_up():
        slot = me if every else lax.rem(me, n_tiles)
        total = parts[slot]
        for d, (peer, copy) in enumerate(part_copies, 1):
            copy.wait_recv()
            total = total + parts_in[wide_peer(n_wide - d)]
        value = total[:8] / (total[8:] + 1.0)
        tile[...] = value
        for source, copy in tile_copies:
            copy.start()
        tiles_in[slot] = value

    def send_tile():
        when(owner(me))(add_up)

    def finish():
        for source, copy in tile_copies:
            when(owner(source))(copy.wait_recv)
        for t in range(n_tiles):
            space, row, span = where_is(t)
            book_ref[space, row : row + 8, span] = tiles_in[t]

    def refits(first, last):
        def run():
            for space in range(first, last):
                refit(space)

        return run

    beside = [refits(i * spaces // 4, (i + 1) * spaces // 4) for i in range(4)]
    beside += [send_sums, None, send_parts, None, send_tile]
    for turn in range(chunks + stages - 1):
        for j in range(stages):
            q = turn - j
            if 0 <= q < chunks:
                if beside:
                    task = beside.pop(0)
                    if task is not None:
                        task()
                advance(j, q)
    for task in beside:
        if task is not None:
            task()
    finish()
    for copy in sub_copies.values():
        copy.wait_recv()

    for copy in [*len_copies, *wide_copies.values(), *sub_copies.values(), *sum_copies]:
        copy.wait_send()
    for peer, copy in part_copies:
        when(owner(peer))(copy.wait_send)

    def drain():
        for source, copy in tile_copies:
            copy.wait_send()

    when(owner(me))(drain)


def solution(mesh):
    n_wide, n_sub = mesh.shape["wide"], mesh.shape["sub"]
    stages = n_wide.bit_length() - 1

    def body(lengths, postings, codes, rotation):
        capacity, dims = postings.shape[1:]
        spaces = codes.shape[1]
        shard = capacity // 2
        width = 256
        chunks = shard // width
        height = dims
        own_dims, own_spaces = dims // n_sub, spaces // n_sub
        n_tiles = own_spaces * (SUBDIM // 8) * (KCODES // LANES)
        bf16, f32 = jnp.bfloat16, jnp.float32
        vmem = pl.BlockSpec(memory_space=pltpu.VMEM)
        dma = pltpu.SemaphoreType.DMA
        return pl.pallas_call(
            functools.partial(kernel, n_wide, n_sub),
            out_shape=(
                jax.ShapeDtypeStruct((n_sub, own_dims, shard), bf16),
                jax.ShapeDtypeStruct((own_spaces, SUBDIM, KCODES), f32),
            ),
            in_specs=[pl.BlockSpec(memory_space=pltpu.HBM)] * 4,
            out_specs=(vmem, vmem),
            scratch_shapes=[
                pltpu.VMEM(postings.shape, bf16),
                pltpu.VMEM(codes.shape, jnp.int32),
                pltpu.VMEM(rotation.shape, bf16),
                pltpu.VMEM((n_wide, *lengths.shape), jnp.int32),
                pltpu.VMEM((capacity // LANES, height, LANES), bf16),
                pltpu.VMEM((stages, 2, chunks, height, width), bf16),
                pltpu.VMEM((stages, chunks, height, width), bf16),
                pltpu.VMEM((chunks, n_sub, own_dims, width), bf16),
                pltpu.VMEM((n_sub, own_spaces, SUBDIM + 8, KCODES), f32),
                pltpu.VMEM((n_sub, own_spaces, SUBDIM + 8, KCODES), f32),
                pltpu.VMEM((own_spaces, SUBDIM + 8, KCODES), f32),
                pltpu.VMEM((n_tiles, 16, LANES), f32),
                pltpu.VMEM((n_wide, 16, LANES), f32),
                pltpu.VMEM((8, LANES), f32),
                pltpu.VMEM((n_tiles, 8, LANES), f32),
                dma((n_wide,)),
                dma((n_wide,)),
                dma((stages, chunks)),
                dma((stages, chunks)),
                dma((chunks, n_sub)),
                dma((chunks, n_sub)),
                dma((n_sub,)),
                dma((n_sub,)),
                dma((n_wide,)),
                dma((n_wide,)),
                dma((n_wide,)),
                dma((n_wide,)),
                dma((4,)),
            ],
            compiler_params=pltpu.CompilerParams(
                collective_id=0, has_side_effects=True, vmem_limit_bytes=60 * 1024 * 1024
            ),
        )(lengths, postings, codes, rotation)

    return jax.shard_map(
        body,
        mesh=mesh,
        in_specs=(P("sub", "wide"), P("sub", "wide", None), P("sub", None, "wide"), P()),
        out_specs=(P(None, "sub", "wide"), P("sub", None, None)),
        check_vma=False,
    )
```

```python
import functools

import jax
import jax.numpy as jnp
from jax import lax
from jax.experimental import pallas as pl
from jax.experimental.pallas import tpu as pltpu
from jax.sharding import PartitionSpec as P

KCODES = 256
SUBDIM = 16
LANES = 128
MESH = pl.DeviceIdType.MESH
NT = (((1,), (1,)), ((), ()))


def when(condition):
    if condition is True:
        return lambda body: body()
    return pl.when(condition)


def kernel(
    n_wide,
    n_sub,
    len_ref,
    post_hbm,
    code_hbm,
    rot_hbm,
    out_ref,
    book_ref,
    post_ref,
    code_ref,
    rot_ref,
    lens,
    local,
    halves,
    arrived,
    final,
    sums,
    sums_in,
    acc,
    parts,
    parts_in,
    tile,
    tiles_in,
    len_send,
    len_recv,
    wide_send,
    wide_recv,
    sub_send,
    sub_recv,
    sum_send,
    sum_recv,
    part_send,
    part_recv,
    tile_send,
    tile_recv,
    load,
):
    me = lax.axis_index("wide")
    sub = lax.axis_index("sub")
    stages = n_wide.bit_length() - 1
    capacity, dims = post_ref.shape[1], post_ref.shape[2]
    spaces = code_ref.shape[1]
    shard = capacity // 2
    chunks, height, width = halves.shape[2:]
    own_dims = dims // n_sub
    own_spaces = spaces // n_sub
    n_tiles = parts.shape[0]
    columns = KCODES // LANES

    def wide_peer(distance):
        return lax.rem(me + distance, n_wide)

    def sub_peer(distance):
        return lax.rem(sub + distance, n_sub)

    loads = [
        pltpu.make_async_copy(source, target, load.at[i])
        for i, (source, target) in enumerate(
            ((rot_hbm, rot_ref), (post_hbm, post_ref), (code_hbm, code_ref), (len_ref, lens.at[me]))
        )
    ]
    for copy in loads:
        copy.start()
    barrier = pltpu.get_barrier_semaphore()
    for d in range(1, n_wide):
        pl.semaphore_signal(barrier, inc=1, device_id=(wide_peer(d), sub), device_id_type=MESH)
    for d in range(1, n_sub):
        pl.semaphore_signal(barrier, inc=1, device_id=(me, sub_peer(d)), device_id_type=MESH)
    pl.semaphore_wait(barrier, n_wide + n_sub - 2)

    len_copies = []
    for d in range(1, n_wide):
        copy = pltpu.make_async_remote_copy(
            src_ref=len_ref,
            dst_ref=lens.at[me],
            send_sem=len_send.at[d],
            recv_sem=len_recv.at[d],
            device_id=(wide_peer(d), sub),
            device_id_type=MESH,
        )
        copy.start()
        len_copies.append(copy)

    loads[0].wait()
    turned = rot_ref[...].astype(jnp.float32).T.astype(jnp.bfloat16)
    blocks = capacity // LANES
    step = capacity // 4
    loads[1].wait()
    for i in range(4):
        span = slice(i * step, (i + 1) * step)
        block = lax.dot_general(turned, post_ref[0, span, :], NT, preferred_element_type=jnp.float32)
        block = block.astype(jnp.bfloat16)
        for k in range(step // LANES):
            local[i * (step // LANES) + k] = block[:, k * LANES : (k + 1) * LANES]
    loads[2].wait()
    loads[3].wait()
    for copy in len_copies:
        copy.wait_recv()
    all_lens = lens[...].reshape(n_wide, lens.shape[2])
    device = lax.broadcasted_iota(jnp.int32, all_lens.shape, 0)

    def start_of(index):
        return jnp.sum(jnp.where(device < index, all_lens, 0))

    mine = start_of(me)
    rest = lax.rem(n_wide * capacity - mine, LANES)
    across = lax.broadcasted_iota(jnp.int32, (2 * LANES, LANES), 0) - lax.broadcasted_iota(
        jnp.int32, (2 * LANES, LANES), 1
    )
    shift = jnp.where(across == rest, 1.0, 0.0).astype(jnp.bfloat16)

    def placed(half):
        first = lax.rem(half * shard - mine + n_wide * capacity, capacity) // LANES
        loaded = [local[lax.rem(first + k, blocks)] for k in range(shard // LANES + 1)]
        pairs = [jnp.concatenate(loaded[k : k + 2], axis=1) for k in range(shard // LANES)]
        moved = jnp.dot(
            jnp.concatenate(pairs, axis=0), shift, preferred_element_type=jnp.float32
        ).astype(jnp.bfloat16)
        moved = [moved[k * height : (k + 1) * height] for k in range(shard // LANES)]
        each = width // LANES
        return [jnp.concatenate(moved[q * each : (q + 1) * each], axis=1) for q in range(chunks)]

    def bit(j):
        return lax.rem(me // (1 << j), 2)

    wide_copies = {}

    def send_wide(j, q):
        copy = pltpu.make_async_remote_copy(
            src_ref=halves.at[j, 0, q],
            dst_ref=arrived.at[j, q],
            send_sem=wide_send.at[j, q],
            recv_sem=wide_recv.at[j, q],
            device_id=(me + (1 << j) - (2 << j) * bit(j), sub),
            device_id_type=MESH,
        )
        copy.start()
        wide_copies[j, q] = copy

    for q, piece in enumerate(placed(1 - bit(0))):
        halves[0, 0, q] = piece
        send_wide(0, q)
    for q, piece in enumerate(placed(bit(0))):
        halves[0, 1, q] = piece

    edges = []
    for j in range(stages):
        group = me - lax.rem(me, 2 << j)
        edges.append((start_of(group), start_of(group + (1 << j))))

    lane = lax.broadcasted_iota(jnp.int32, (height, width), 1)

    def pick(j, q, position):
        below = jnp.where(position < edges[j][1], 1, 0) + bit(j)
        return jnp.where(below == 1, halves[j, 1, q], arrived[j, q])

    sub_copies = {}

    def advance(j, q):
        wide_copies[j, q].wait_recv()
        if j < stages - 1:
            low = lax.rem(me, 2 << j) * shard + q * width
            first = edges[j][0]

            def position(half):
                offset = half * ((2 << j) * shard) + low - first
                return first + jnp.bitwise_and(offset + lane, (4 << j) * shard - 1)

            halves[j + 1, 0, q] = pick(j, q, position(1 - bit(j + 1)))
            send_wide(j + 1, q)
            halves[j + 1, 1, q] = pick(j, q, position(bit(j + 1)))
            return
        rows = pick(j, q, me * shard + q * width + lane)
        for s in range(n_sub):
            final[q, s] = rows[s * own_dims : (s + 1) * own_dims]
        span = pl.ds(q * width, width)
        for d in range(1, n_sub):
            copy = pltpu.make_async_remote_copy(
                src_ref=final.at[q, sub_peer(d)],
                dst_ref=out_ref.at[sub, :, span],
                send_sem=sub_send.at[q, d],
                recv_sem=sub_recv.at[q, d],
                device_id=(me, sub_peer(d)),
                device_id_type=MESH,
            )
            copy.start()
            sub_copies[q, d] = copy
        out_ref[sub, :, span] = final[q, sub]

    pieces = 4
    part_slots = capacity // pieces
    centroid = lax.broadcasted_iota(jnp.int32, (KCODES, part_slots), 0)
    slot = lax.broadcasted_iota(jnp.int32, (spaces, capacity), 1)
    ones = jnp.ones((SUBDIM, part_slots), jnp.bfloat16)
    code_ref[0] = jnp.where(slot < start_of(me + 1) - mine, code_ref[0], -1)

    def refit(space):
        total = None
        for i in range(pieces):
            span = slice(i * part_slots, (i + 1) * part_slots)
            labels = code_ref[0, space : space + 1, span]
            onehot = jnp.where(centroid == labels, 1.0, 0.0).astype(jnp.bfloat16)
            each = part_slots // LANES
            values = [
                local[i * each + k, space * SUBDIM : (space + 1) * SUBDIM] for k in range(each)
            ]
            left = jnp.concatenate([jnp.concatenate(values, axis=1), ones], axis=0)
            part = lax.dot_general(left, onehot, NT, preferred_element_type=jnp.float32)
            total = part if total is None else total + part
        sums[space // own_spaces, space % own_spaces] = total[: SUBDIM + 8]

    sum_copies = []

    def send_sums():
        for d in range(1, n_sub):
            copy = pltpu.make_async_remote_copy(
                src_ref=sums.at[sub_peer(d)],
                dst_ref=sums_in.at[sub],
                send_sem=sum_send.at[d],
                recv_sem=sum_recv.at[d],
                device_id=(me, sub_peer(d)),
                device_id_type=MESH,
            )
            copy.start()
            sum_copies.append(copy)

    def where_is(t):
        space, rest = divmod(t, 2 * columns)
        row, column = divmod(rest, columns)
        return space, row * 8, slice(column * LANES, (column + 1) * LANES)

    every = n_tiles == n_wide

    def owner(index):
        return True if every else index < n_tiles

    part_copies = []

    def send_parts():
        for d, copy in enumerate(sum_copies, 1):
            copy.wait_recv()
        total = sums[sub]
        for d in range(1, n_sub):
            total = total + sums_in[sub_peer(n_sub - d)]
        acc[...] = total
        for t in range(n_tiles):
            space, row, span = where_is(t)
            parts[t, :8] = acc[space, row : row + 8, span]
            parts[t, 8:] = acc[space, SUBDIM : SUBDIM + 8, span]
        for d in range(1, n_wide):
            peer = wide_peer(d)
            copy = pltpu.make_async_remote_copy(
                src_ref=parts.at[peer if every else lax.rem(peer, n_tiles)],
                dst_ref=parts_in.at[me],
                send_sem=part_send.at[d],
                recv_sem=part_recv.at[d],
                device_id=(peer, sub),
                device_id_type=MESH,
            )
            when(owner(peer))(copy.start)
            part_copies.append((peer, copy))

    tile_copies = []
    for d in range(1, n_wide):
        slot = me if every else lax.rem(me, n_tiles)
        copy = pltpu.make_async_remote_copy(
            src_ref=tile,
            dst_ref=tiles_in.at[slot],
            send_sem=tile_send.at[d],
            recv_sem=tile_recv.at[d],
            device_id=(wide_peer(d), sub),
            device_id_type=MESH,
        )
        tile_copies.append((wide_peer(n_wide - d), copy))

    def add_up():
        slot = me if every else lax.rem(me, n_tiles)
        total = parts[slot]
        for d, (peer, copy) in enumerate(part_copies, 1):
            copy.wait_recv()
            total = total + parts_in[wide_peer(n_wide - d)]
        value = total[:8] / (total[8:] + 1.0)
        tile[...] = value
        for source, copy in tile_copies:
            copy.start()
        tiles_in[slot] = value

    def send_tile():
        when(owner(me))(add_up)

    def finish():
        for source, copy in tile_copies:
            when(owner(source))(copy.wait_recv)
        for t in range(n_tiles):
            space, row, span = where_is(t)
            book_ref[space, row : row + 8, span] = tiles_in[t]

    def refits(first, last):
        def run():
            for space in range(first, last):
                refit(space)

        return run

    beside = [refits(i * spaces // 4, (i + 1) * spaces // 4) for i in range(4)]
    beside += [send_sums, None, send_parts, None, send_tile]
    for j, q in ((j, q) for j in range(stages) for q in range(chunks)):
        if beside:
            task = beside.pop(0)
            if task is not None:
                task()
        advance(j, q)
    for task in beside:
        if task is not None:
            task()
    finish()
    for copy in sub_copies.values():
        copy.wait_recv()

    for copy in [*len_copies, *wide_copies.values(), *sub_copies.values(), *sum_copies]:
        copy.wait_send()
    for peer, copy in part_copies:
        when(owner(peer))(copy.wait_send)

    def drain():
        for source, copy in tile_copies:
            copy.wait_send()

    when(owner(me))(drain)


def solution(mesh):
    n_wide, n_sub = mesh.shape["wide"], mesh.shape["sub"]
    stages = n_wide.bit_length() - 1

    def body(lengths, postings, codes, rotation):
        capacity, dims = postings.shape[1:]
        spaces = codes.shape[1]
        shard = capacity // 2
        width = 256
        chunks = shard // width
        height = dims
        own_dims, own_spaces = dims // n_sub, spaces // n_sub
        n_tiles = own_spaces * (SUBDIM // 8) * (KCODES // LANES)
        bf16, f32 = jnp.bfloat16, jnp.float32
        vmem = pl.BlockSpec(memory_space=pltpu.VMEM)
        dma = pltpu.SemaphoreType.DMA
        return pl.pallas_call(
            functools.partial(kernel, n_wide, n_sub),
            out_shape=(
                jax.ShapeDtypeStruct((n_sub, own_dims, shard), bf16),
                jax.ShapeDtypeStruct((own_spaces, SUBDIM, KCODES), f32),
            ),
            in_specs=[pl.BlockSpec(memory_space=pltpu.HBM)] * 4,
            out_specs=(vmem, vmem),
            scratch_shapes=[
                pltpu.VMEM(postings.shape, bf16),
                pltpu.VMEM(codes.shape, jnp.int32),
                pltpu.VMEM(rotation.shape, bf16),
                pltpu.VMEM((n_wide, *lengths.shape), jnp.int32),
                pltpu.VMEM((capacity // LANES, height, LANES), bf16),
                pltpu.VMEM((stages, 2, chunks, height, width), bf16),
                pltpu.VMEM((stages, chunks, height, width), bf16),
                pltpu.VMEM((chunks, n_sub, own_dims, width), bf16),
                pltpu.VMEM((n_sub, own_spaces, SUBDIM + 8, KCODES), f32),
                pltpu.VMEM((n_sub, own_spaces, SUBDIM + 8, KCODES), f32),
                pltpu.VMEM((own_spaces, SUBDIM + 8, KCODES), f32),
                pltpu.VMEM((n_tiles, 16, LANES), f32),
                pltpu.VMEM((n_wide, 16, LANES), f32),
                pltpu.VMEM((8, LANES), f32),
                pltpu.VMEM((n_tiles, 8, LANES), f32),
                dma((n_wide,)),
                dma((n_wide,)),
                dma((stages, chunks)),
                dma((stages, chunks)),
                dma((chunks, n_sub)),
                dma((chunks, n_sub)),
                dma((n_sub,)),
                dma((n_sub,)),
                dma((n_wide,)),
                dma((n_wide,)),
                dma((n_wide,)),
                dma((n_wide,)),
                dma((4,)),
            ],
            compiler_params=pltpu.CompilerParams(
                collective_id=0, has_side_effects=True, vmem_limit_bytes=60 * 1024 * 1024
            ),
        )(lengths, postings, codes, rotation)

    return jax.shard_map(
        body,
        mesh=mesh,
        in_specs=(P("sub", "wide"), P("sub", "wide", None), P("sub", None, "wide"), P()),
        out_specs=(P(None, "sub", "wide"), P("sub", None, None)),
        check_vma=False,
    )
```

```python
import functools

import jax
import jax.numpy as jnp
from jax import lax
from jax.experimental import pallas as pl
from jax.experimental.pallas import tpu as pltpu
from jax.sharding import PartitionSpec as P

KCODES = 256
SUBDIM = 16
LANES = 128
MESH = pl.DeviceIdType.MESH
NT = (((1,), (1,)), ((), ()))


def when(condition):
    if condition is True:
        return lambda body: body()
    return pl.when(condition)


def kernel(
    n_wide,
    n_sub,
    len_ref,
    post_hbm,
    code_hbm,
    rot_hbm,
    out_ref,
    book_ref,
    post_ref,
    code_ref,
    rot_ref,
    lens,
    local,
    halves,
    arrived,
    final,
    sums,
    sums_in,
    acc,
    parts,
    parts_in,
    tile,
    tiles_in,
    len_send,
    len_recv,
    wide_send,
    wide_recv,
    sub_send,
    sub_recv,
    sum_send,
    sum_recv,
    part_send,
    part_recv,
    tile_send,
    tile_recv,
    load,
):
    me = lax.axis_index("wide")
    sub = lax.axis_index("sub")
    stages = n_wide.bit_length() - 1
    capacity, dims = post_ref.shape[1], post_ref.shape[2]
    spaces = code_ref.shape[1]
    shard = capacity // 2
    chunks, height, width = halves.shape[2:]
    own_dims = dims // n_sub
    own_spaces = spaces // n_sub
    n_tiles = parts.shape[0]
    columns = KCODES // LANES

    def wide_peer(distance):
        return lax.rem(me + distance, n_wide)

    def sub_peer(distance):
        return lax.rem(sub + distance, n_sub)

    loads = [
        pltpu.make_async_copy(source, target, load.at[i])
        for i, (source, target) in enumerate(
            ((rot_hbm, rot_ref), (post_hbm, post_ref), (code_hbm, code_ref), (len_ref, lens.at[me]))
        )
    ]
    for copy in loads:
        copy.start()
    barrier = pltpu.get_barrier_semaphore()
    for d in range(1, n_wide):
        pl.semaphore_signal(barrier, inc=1, device_id=(wide_peer(d), sub), device_id_type=MESH)
    for d in range(1, n_sub):
        pl.semaphore_signal(barrier, inc=1, device_id=(me, sub_peer(d)), device_id_type=MESH)
    pl.semaphore_wait(barrier, n_wide + n_sub - 2)

    len_copies = []
    for d in range(1, n_wide):
        copy = pltpu.make_async_remote_copy(
            src_ref=len_ref,
            dst_ref=lens.at[me],
            send_sem=len_send.at[d],
            recv_sem=len_recv.at[d],
            device_id=(wide_peer(d), sub),
            device_id_type=MESH,
        )
        copy.start()
        len_copies.append(copy)

    loads[0].wait()
    turned = rot_ref[...].astype(jnp.float32).T.astype(jnp.bfloat16)
    blocks = capacity // LANES
    step = capacity // 4
    loads[1].wait()
    for i in range(4):
        span = slice(i * step, (i + 1) * step)
        block = lax.dot_general(turned, post_ref[0, span, :], NT, preferred_element_type=jnp.float32)
        block = block.astype(jnp.bfloat16)
        for k in range(step // LANES):
            local[i * (step // LANES) + k] = block[:, k * LANES : (k + 1) * LANES]
    loads[2].wait()
    loads[3].wait()
    pieces = 4
    part_slots = capacity // pieces
    centroid = lax.broadcasted_iota(jnp.int32, (KCODES, part_slots), 0)
    slot = lax.broadcasted_iota(jnp.int32, (spaces, capacity), 1)
    ones = jnp.ones((SUBDIM, part_slots), jnp.bfloat16)
    code_ref[0] = jnp.where(slot < jnp.sum(lens[me]), code_ref[0], -1)

    def refit(space):
        total = None
        for i in range(pieces):
            span = slice(i * part_slots, (i + 1) * part_slots)
            labels = code_ref[0, space : space + 1, span]
            onehot = jnp.where(centroid == labels, 1.0, 0.0).astype(jnp.bfloat16)
            each = part_slots // LANES
            values = [
                local[i * each + k, space * SUBDIM : (space + 1) * SUBDIM] for k in range(each)
            ]
            left = jnp.concatenate([jnp.concatenate(values, axis=1), ones], axis=0)
            part = lax.dot_general(left, onehot, NT, preferred_element_type=jnp.float32)
            total = part if total is None else total + part
        sums[space // own_spaces, space % own_spaces] = total[: SUBDIM + 8]

    sum_copies = []

    def send_sums():
        for d in range(1, n_sub):
            copy = pltpu.make_async_remote_copy(
                src_ref=sums.at[sub_peer(d)],
                dst_ref=sums_in.at[sub],
                send_sem=sum_send.at[d],
                recv_sem=sum_recv.at[d],
                device_id=(me, sub_peer(d)),
                device_id_type=MESH,
            )
            copy.start()
            sum_copies.append(copy)

    for space in range(spaces):
        refit(space)
    send_sums()

    for copy in len_copies:
        copy.wait_recv()
    all_lens = lens[...].reshape(n_wide, lens.shape[2])
    device = lax.broadcasted_iota(jnp.int32, all_lens.shape, 0)

    def start_of(index):
        return jnp.sum(jnp.where(device < index, all_lens, 0))

    mine = start_of(me)
    rest = lax.rem(n_wide * capacity - mine, LANES)
    across = lax.broadcasted_iota(jnp.int32, (2 * LANES, LANES), 0) - lax.broadcasted_iota(
        jnp.int32, (2 * LANES, LANES), 1
    )
    shift = jnp.where(across == rest, 1.0, 0.0).astype(jnp.bfloat16)

    def placed(half):
        first = lax.rem(half * shard - mine + n_wide * capacity, capacity) // LANES
        loaded = [local[lax.rem(first + k, blocks)] for k in range(shard // LANES + 1)]
        pairs = [jnp.concatenate(loaded[k : k + 2], axis=1) for k in range(shard // LANES)]
        moved = jnp.dot(
            jnp.concatenate(pairs, axis=0), shift, preferred_element_type=jnp.float32
        ).astype(jnp.bfloat16)
        moved = [moved[k * height : (k + 1) * height] for k in range(shard // LANES)]
        each = width // LANES
        return [jnp.concatenate(moved[q * each : (q + 1) * each], axis=1) for q in range(chunks)]

    def bit(j):
        return lax.rem(me // (1 << j), 2)

    wide_copies = {}

    def send_wide(j, q):
        copy = pltpu.make_async_remote_copy(
            src_ref=halves.at[j, 0, q],
            dst_ref=arrived.at[j, q],
            send_sem=wide_send.at[j, q],
            recv_sem=wide_recv.at[j, q],
            device_id=(me + (1 << j) - (2 << j) * bit(j), sub),
            device_id_type=MESH,
        )
        copy.start()
        wide_copies[j, q] = copy

    for q, piece in enumerate(placed(1 - bit(0))):
        halves[0, 0, q] = piece
        send_wide(0, q)
    for q, piece in enumerate(placed(bit(0))):
        halves[0, 1, q] = piece

    edges = []
    for j in range(stages):
        group = me - lax.rem(me, 2 << j)
        edges.append((start_of(group), start_of(group + (1 << j))))

    lane = lax.broadcasted_iota(jnp.int32, (height, width), 1)

    def pick(j, q, position):
        below = jnp.where(position < edges[j][1], 1, 0) + bit(j)
        return jnp.where(below == 1, halves[j, 1, q], arrived[j, q])

    sub_copies = {}

    def advance(j, q):
        wide_copies[j, q].wait_recv()
        if j < stages - 1:
            low = lax.rem(me, 2 << j) * shard + q * width
            first = edges[j][0]

            def position(half):
                offset = half * ((2 << j) * shard) + low - first
                return first + jnp.bitwise_and(offset + lane, (4 << j) * shard - 1)

            halves[j + 1, 0, q] = pick(j, q, position(1 - bit(j + 1)))
            send_wide(j + 1, q)
            halves[j + 1, 1, q] = pick(j, q, position(bit(j + 1)))
            return
        rows = pick(j, q, me * shard + q * width + lane)
        for s in range(n_sub):
            final[q, s] = rows[s * own_dims : (s + 1) * own_dims]
        span = pl.ds(q * width, width)
        for d in range(1, n_sub):
            copy = pltpu.make_async_remote_copy(
                src_ref=final.at[q, sub_peer(d)],
                dst_ref=out_ref.at[sub, :, span],
                send_sem=sub_send.at[q, d],
                recv_sem=sub_recv.at[q, d],
                device_id=(me, sub_peer(d)),
                device_id_type=MESH,
            )
            copy.start()
            sub_copies[q, d] = copy
        out_ref[sub, :, span] = final[q, sub]

    def where_is(t):
        space, rest = divmod(t, 2 * columns)
        row, column = divmod(rest, columns)
        return space, row * 8, slice(column * LANES, (column + 1) * LANES)

    every = n_tiles == n_wide

    def owner(index):
        return True if every else index < n_tiles

    part_copies = []

    def send_parts():
        for d, copy in enumerate(sum_copies, 1):
            copy.wait_recv()
        total = sums[sub]
        for d in range(1, n_sub):
            total = total + sums_in[sub_peer(n_sub - d)]
        acc[...] = total
        for t in range(n_tiles):
            space, row, span = where_is(t)
            parts[t, :8] = acc[space, row : row + 8, span]
            parts[t, 8:] = acc[space, SUBDIM : SUBDIM + 8, span]
        for d in range(1, n_wide):
            peer = wide_peer(d)
            copy = pltpu.make_async_remote_copy(
                src_ref=parts.at[peer if every else lax.rem(peer, n_tiles)],
                dst_ref=parts_in.at[me],
                send_sem=part_send.at[d],
                recv_sem=part_recv.at[d],
                device_id=(peer, sub),
                device_id_type=MESH,
            )
            when(owner(peer))(copy.start)
            part_copies.append((peer, copy))

    tile_copies = []
    for d in range(1, n_wide):
        slot = me if every else lax.rem(me, n_tiles)
        copy = pltpu.make_async_remote_copy(
            src_ref=tile,
            dst_ref=tiles_in.at[slot],
            send_sem=tile_send.at[d],
            recv_sem=tile_recv.at[d],
            device_id=(wide_peer(d), sub),
            device_id_type=MESH,
        )
        tile_copies.append((wide_peer(n_wide - d), copy))

    def add_up():
        slot = me if every else lax.rem(me, n_tiles)
        total = parts[slot]
        for d, (peer, copy) in enumerate(part_copies, 1):
            copy.wait_recv()
            total = total + parts_in[wide_peer(n_wide - d)]
        value = total[:8] / (total[8:] + 1.0)
        tile[...] = value
        for source, copy in tile_copies:
            copy.start()
        tiles_in[slot] = value

    def send_tile():
        when(owner(me))(add_up)

    def finish():
        for source, copy in tile_copies:
            when(owner(source))(copy.wait_recv)
        for t in range(n_tiles):
            space, row, span = where_is(t)
            book_ref[space, row : row + 8, span] = tiles_in[t]

    beside = [None, None, None, None, send_parts, None, None, send_tile]
    for j, q in ((j, q) for j in range(stages) for q in range(chunks)):
        if beside:
            task = beside.pop(0)
            if task is not None:
                task()
        advance(j, q)
    for task in beside:
        if task is not None:
            task()
    finish()
    for copy in sub_copies.values():
        copy.wait_recv()

    for copy in [*len_copies, *wide_copies.values(), *sub_copies.values(), *sum_copies]:
        copy.wait_send()
    for peer, copy in part_copies:
        when(owner(peer))(copy.wait_send)

    def drain():
        for source, copy in tile_copies:
            copy.wait_send()

    when(owner(me))(drain)


def solution(mesh):
    n_wide, n_sub = mesh.shape["wide"], mesh.shape["sub"]
    stages = n_wide.bit_length() - 1

    def body(lengths, postings, codes, rotation):
        capacity, dims = postings.shape[1:]
        spaces = codes.shape[1]
        shard = capacity // 2
        width = 256
        chunks = shard // width
        height = dims
        own_dims, own_spaces = dims // n_sub, spaces // n_sub
        n_tiles = own_spaces * (SUBDIM // 8) * (KCODES // LANES)
        bf16, f32 = jnp.bfloat16, jnp.float32
        vmem = pl.BlockSpec(memory_space=pltpu.VMEM)
        dma = pltpu.SemaphoreType.DMA
        return pl.pallas_call(
            functools.partial(kernel, n_wide, n_sub),
            out_shape=(
                jax.ShapeDtypeStruct((n_sub, own_dims, shard), bf16),
                jax.ShapeDtypeStruct((own_spaces, SUBDIM, KCODES), f32),
            ),
            in_specs=[pl.BlockSpec(memory_space=pltpu.HBM)] * 4,
            out_specs=(vmem, vmem),
            scratch_shapes=[
                pltpu.VMEM(postings.shape, bf16),
                pltpu.VMEM(codes.shape, jnp.int32),
                pltpu.VMEM(rotation.shape, bf16),
                pltpu.VMEM((n_wide, *lengths.shape), jnp.int32),
                pltpu.VMEM((capacity // LANES, height, LANES), bf16),
                pltpu.VMEM((stages, 2, chunks, height, width), bf16),
                pltpu.VMEM((stages, chunks, height, width), bf16),
                pltpu.VMEM((chunks, n_sub, own_dims, width), bf16),
                pltpu.VMEM((n_sub, own_spaces, SUBDIM + 8, KCODES), f32),
                pltpu.VMEM((n_sub, own_spaces, SUBDIM + 8, KCODES), f32),
                pltpu.VMEM((own_spaces, SUBDIM + 8, KCODES), f32),
                pltpu.VMEM((n_tiles, 16, LANES), f32),
                pltpu.VMEM((n_wide, 16, LANES), f32),
                pltpu.VMEM((8, LANES), f32),
                pltpu.VMEM((n_tiles, 8, LANES), f32),
                dma((n_wide,)),
                dma((n_wide,)),
                dma((stages, chunks)),
                dma((stages, chunks)),
                dma((chunks, n_sub)),
                dma((chunks, n_sub)),
                dma((n_sub,)),
                dma((n_sub,)),
                dma((n_wide,)),
                dma((n_wide,)),
                dma((n_wide,)),
                dma((n_wide,)),
                dma((4,)),
            ],
            compiler_params=pltpu.CompilerParams(
                collective_id=0, has_side_effects=True, vmem_limit_bytes=60 * 1024 * 1024
            ),
        )(lengths, postings, codes, rotation)

    return jax.shard_map(
        body,
        mesh=mesh,
        in_specs=(P("sub", "wide"), P("sub", "wide", None), P("sub", None, "wide"), P()),
        out_specs=(P(None, "sub", "wide"), P("sub", None, None)),
        check_vma=False,
    )
```
